32 devices in a mesh: groups: 2 (over y), sky: 16 (over z, x, core).
Axes of the slice: x: 2, y: 2, z: 4, core: 2. Of those that a mesh axis runs over, the one named last changes fastest.
Arguments:
- wigner: bfloat16 [32, 2, 32, 64, 2048], P('sky'), may hold values from -1 to 1
- sky_blocks: bfloat16 [32, 2, 64, 2048], P('sky'), may hold values from -0.059814453 to 0.059814453
- beam: bfloat16 [2048, 8192], P('sky', 'groups'), parts along dimension 1, may hold values from -0.059814453 to 0.059814453
- block_order: int32 [32], replicated, may hold values from 0 to 31, each once
- pointing: int32 [256, 1024], P(('groups', 'sky')), parts along dimension 0, may hold values from 0 to 524287
Outputs:
- timestream: float32 [256, 1024], P(('groups', 'sky')), parts along dimension 0
The draws below stay inside these ranges and needn't reach their ends.
There are 2 independent parts, one for each index of `groups`. The reference program is written for one: setup_inputs(seed, part) draws one part's arguments, and reference() takes and returns one part's arrays. A program takes and returns all parts, laid end to end along the dimension named above; an argument that names none is the same for every part. Nothing has to cross between parts.
Inputs may be any that keep to these rules, and one draw needn't show every extreme that they name: `block_order`: each of the 32 m-blocks is listed exactly once.
All inputs are finite; a program needn't handle non-finite values.
Results may differ from the reference program's by a relative error of at most 0.0048.
Values may be sent and summed in bfloat16 or wider, within the bound.
A program may use at most 320 MiB of HBM per device.

```python
import math
import jax
import jax.numpy as jnp
from jax import lax

L = 2048
K = 32
CYCLES = 2
DET = 64
NSR = 1024
NB = 32
MB = 64
PAIRS = 128
NPHI = 4096
NPSI = 128


def touch_ends(entries, stream_key, low, largest):
    longest = entries.shape.index(max(entries.shape))
    spots = []
    for shift in (0, 1):
        where = [jax.random.randint(jax.random.fold_in(stream_key, axis), (), 0, length) for axis, length in enumerate(entries.shape)]
        where[longest] = (where[longest] + shift) % entries.shape[longest]
        spots.append(tuple(where))
    return entries.at[spots[0]].set(low).at[spots[1]].set(largest)


def steps_of(own_key, shape, split, smallest, top_value):
    gain = 1.0
    for dim, blocks in split:
        steps = jax.random.uniform(jax.random.fold_in(jax.random.fold_in(own_key, 6), dim), (blocks,), jnp.float32, smallest / len(split), top_value / len(split))
        gain = gain * jnp.repeat(jnp.exp(steps), shape[dim] // blocks).reshape((-1,) + (1,) * (len(shape) - 1 - dim))
    return gain


def scatter_about(key, extent, spread, limit, cuts=(), held_as=jnp.bfloat16):
    values = jax.random.normal(key, extent, jnp.float32) * spread
    if len(cuts) > 0:
        values = steps_of(key, extent, cuts, -0.22, 0.18) * values
    return jnp.clip(values, min=-limit, max=limit).astype(held_as)


def setup_inputs(seed: int = 0, part: int = 0) -> dict:
    key_list = jax.random.split(jax.random.key(seed), 6)
    part_splits = jax.random.split(jax.random.fold_in(key_list[5], part), 6)
    wigner = jnp.clip(jax.random.uniform(key_list[0], (NB, CYCLES, K, MB, L), jnp.float32, -1.0, 1.0) * steps_of(key_list[0], (NB, CYCLES, K, MB, L), ((0, 16),), -0.4, 0.0), -1.0, 1.0).astype(jnp.bfloat16)
    sky_blocks = scatter_about(key_list[1], (NB, 2, MB, L), 0.01, 0.059814453, ((0, 16),))
    beam = scatter_about(part_splits[2], (L, 2 * DET * K), 0.01, 0.059814453, ((0, 16),))
    block_order = jax.random.permutation(key_list[3], NB).astype(jnp.int32)
    pointing = touch_ends(jax.random.randint(part_splits[4], (PAIRS, NSR), 0, NPHI * NPSI), jax.random.fold_in(part_splits[4], 1), 0, (NPHI * NPSI) - 1).astype(jnp.int32)
    return dict(wigner=wigner, sky_blocks=sky_blocks, beam=beam, block_order=block_order, pointing=pointing)


def spin_phases(m_values, pixels, cycle_pixels):
    phase_index = (pixels[..., None] * m_values) % cycle_pixels
    angles = phase_index.astype(jnp.float32) * (2.0 * math.pi / cycle_pixels)
    weight = jnp.where(m_values == 0, 1.0, 2.0).astype(jnp.float32)
    return jnp.stack([weight * jnp.cos(angles), weight * jnp.sin(angles)], axis=-2).astype(jnp.bfloat16)


def spin_matrix(spin_sums):
    real_part = spin_sums[..., 0, :, :]
    imag_part = spin_sums[..., 1, :, :]
    upper_half = jnp.stack([real_part, imag_part], axis=-3)
    lower_half = jnp.stack([-imag_part, real_part], axis=-3)
    return jnp.stack([upper_half, lower_half], axis=-4)


def orient_sum(cycle_sum, orients, orient_bins):
    spin_count = cycle_sum.shape[-1]
    k_values = jnp.arange(spin_count, dtype=jnp.int32)
    phase_index = (orients[..., None] * k_values) % orient_bins
    angles = phase_index.astype(jnp.float32) * (2.0 * math.pi / orient_bins)
    weight = jnp.where(k_values == 0, 1.0, 2.0).astype(jnp.float32)
    terms = cycle_sum[..., 0, :] * jnp.cos(angles) - cycle_sum[..., 1, :] * jnp.sin(angles)
    return jnp.sum(weight * terms, axis=-1)


def reference(wigner, sky_blocks, beam, block_order, pointing):
    degree_index = jnp.arange(L, dtype=jnp.int32)
    spin_index = jnp.arange(K, dtype=jnp.int32)
    beam_parts = beam.astype(jnp.float32).reshape(L, 2, DET, K)
    beam_re = beam_parts[:, 0]
    beam_im = beam_parts[:, 1]
    highest = lax.Precision.HIGHEST

    def block_sums(block_item):
        block_table, harmonics, block_id = block_item
        m_values = block_id * MB + jnp.arange(MB, dtype=jnp.int32)
        in_band = (degree_index >= m_values[None, :, None]) & (degree_index >= spin_index[:, None, None])
        table_values = block_table.astype(jnp.float32)
        sky_values = harmonics.astype(jnp.float32)
        coeff_re = jnp.where(in_band, table_values * sky_values[0], 0.0).astype(jnp.bfloat16)
        coeff_im = jnp.where(in_band, table_values * sky_values[1], 0.0).astype(jnp.bfloat16)
        coeff_re = lax.optimization_barrier(coeff_re).astype(jnp.float32)
        coeff_im = lax.optimization_barrier(coeff_im).astype(jnp.float32)
        real_sum = jnp.einsum("rkil,ldk->rdki", coeff_re, beam_re, precision=highest) - jnp.einsum("rkil,ldk->rdki", coeff_im, beam_im, precision=highest)
        imag_sum = jnp.einsum("rkil,ldk->rdki", coeff_re, beam_im, precision=highest) + jnp.einsum("rkil,ldk->rdki", coeff_im, beam_re, precision=highest)
        return jnp.stack([real_sum, imag_sum], axis=2).astype(jnp.bfloat16)

    spin_sums = lax.map(block_sums, (wigner, sky_blocks, block_order))
    spin_sums = jnp.transpose(spin_sums, (1, 2, 3, 4, 0, 5)).reshape(PAIRS, 2, K, NB * MB)
    spin_sums = lax.optimization_barrier(spin_sums)
    m_all = (block_order[:, None] * MB + jnp.arange(MB, dtype=jnp.int32)[None, :]).reshape(-1)
    matrices = spin_matrix(spin_sums)

    def pair_stream(pair_item):
        matrix, point_row = pair_item
        phases = lax.optimization_barrier(spin_phases(m_all, point_row // NPSI, NPHI)).astype(jnp.float32)
        cycle_sum = jnp.einsum("sch,cokh->sok", phases, matrix.astype(jnp.float32), precision=highest)
        return orient_sum(cycle_sum, point_row % NPSI, NPSI)

    return lax.map(pair_stream, (matrices, pointing))
```

```python
import functools
import math

import jax
import jax.numpy as jnp
from jax import lax
from jax.experimental import pallas as pl
from jax.experimental.pallas import tpu as pltpu
from jax.sharding import PartitionSpec as P

CHUNKS = 4
ROWS = 8
VMEM_LIMIT = 48 * 1024 * 1024


def sincos(index, period):
    quarter = period // 4
    index = index & (period - 1)
    shifted = index + quarter // 2
    quadrant = (shifted >> (quarter.bit_length() - 1)) & 3
    rest = (shifted & (quarter - 1)) - quarter // 2
    x = rest.astype(jnp.float32) * (2.0 * math.pi / period)
    y = x * x
    s = x * (1.0 + y * (-1.0 / 6 + y * (1.0 / 120 + y * (-1.0 / 5040 + y * (1.0 / 362880)))))
    c = 1.0 + y * (-0.5 + y * (1.0 / 24 + y * (-1.0 / 720 + y * (1.0 / 40320))))
    odd = (quadrant & 1) == 1
    cos_size = jnp.where(odd, s, c)
    sin_size = jnp.where(odd, c, s)
    cos_value = jnp.where((quadrant == 1) | (quadrant == 2), -cos_size, cos_size)
    sin_value = jnp.where(quadrant >= 2, -sin_size, sin_size)
    return cos_value, sin_value


def phase_kernel(cycle_pixels, orient_bins, pointing_ref, phase_ref, orient_ref):
    samples = pointing_ref.shape[1]
    block_size = phase_ref.shape[1] // 2
    step = cycle_pixels // orient_bins
    low = lax.broadcasted_iota(jnp.int32, (ROWS, samples), 0)
    for j in range(pointing_ref.shape[0]):
        point = pointing_ref[pl.ds(j, 1), :]
        pixel = jnp.broadcast_to(point // orient_bins, (ROWS, samples))
        orient = jnp.broadcast_to(point & (orient_bins - 1), (ROWS, samples))
        base_cos, base_sin = sincos(low * pixel, cycle_pixels)
        if block_size == ROWS:
            cos_rows = [base_cos]
            sin_rows = [base_sin]
        else:
            cos_rows = []
            sin_rows = []
            outer_cos, outer_sin = sincos(low * ROWS * pixel, cycle_pixels)
            for a in range(block_size // ROWS):
                oc = outer_cos[a : a + 1]
                os = outer_sin[a : a + 1]
                cos_rows.append(oc * base_cos - os * base_sin)
                sin_rows.append(os * base_cos + oc * base_sin)
        phase_ref[j] = jnp.concatenate(cos_rows + sin_rows, axis=0).astype(jnp.bfloat16)
        orient_cos, orient_sin = sincos(low * orient * step, cycle_pixels)
        orient_ref[j] = jnp.concatenate([orient_cos, orient_sin], axis=0)


def spin_kernel(first_k, order_ref, wigner_ref, sky_ref, beam_ref, out_ref, coeff):
    blocks, cycles, _, block_size, degrees = wigner_ref.shape
    lanes = beam_ref.shape[-1]
    half = blocks * cycles * block_size
    for b in range(blocks):
        for r in range(cycles):
            table = wigner_ref[b, r, 0]
            row = (b * cycles + r) * block_size
            for c in range(2):
                coeff[c * half + row : c * half + row + block_size, :] = table * sky_ref[b, c]
    beam = beam_ref[...].reshape(degrees, lanes)
    sums = jnp.dot(coeff[...], beam, preferred_element_type=jnp.float32)
    sign = jnp.where(
        lax.broadcasted_iota(jnp.int32, (half, lanes), 1) < lanes // 2, -1.0, 1.0
    ).astype(jnp.float32)
    spin = sums[:half] + sign * pltpu.roll(sums[half:], lanes // 2, 1)
    spin = spin.astype(jnp.bfloat16).astype(jnp.float32)
    k_weight = jnp.where(first_k + pl.program_id(0) == 0, 1.0, 2.0).astype(jnp.float32)
    turned = sign * pltpu.roll(spin, lanes // 2, 1)
    slot = lax.broadcasted_iota(jnp.int32, (block_size, lanes), 0)
    for b in range(blocks):
        weight = jnp.where(order_ref[b] * block_size + slot == 0, 1.0, 2.0) * k_weight
        for r in range(cycles):
            row = (b * cycles + r) * block_size
            both = jnp.concatenate(
                [spin[row : row + block_size] * weight, turned[row : row + block_size] * weight],
                axis=0,
            )
            out_ref[r, b, 0] = both.T


def stream_kernel(first_k, spins, cycle_pixels, orient_bins, detectors, block_size, order_ref,
                  spin_ref, phase_ref, orient_ref, pointing_ref, before_ref, out_ref):
    samples = pointing_ref.shape[1]
    blocks = order_ref.shape[0]
    step = cycle_pixels // orient_bins
    groups = spins // ROWS
    first = pl.program_id(1) * pointing_ref.shape[0]
    row_id = lax.broadcasted_iota(jnp.int32, (max(ROWS, blocks * groups), samples), 0)
    k_outer = (first_k + (row_id % groups) * ROWS) * step
    m_outer = jnp.zeros_like(row_id)
    for b in range(blocks):
        m_outer = jnp.where(row_id // groups == b, order_ref[b] * block_size, m_outer)
    for j in range(pointing_ref.shape[0]):
        point = pointing_ref[pl.ds(j, 1), :]
        pixel = point // orient_bins
        orient = point & (orient_bins - 1)
        outer_cos, outer_sin = sincos(k_outer * orient + m_outer * pixel, cycle_pixels)
        base_cos = orient_ref[j, :ROWS]
        base_sin = orient_ref[j, ROWS:]
        count = blocks * spins
        real_rows = spin_ref[0, pl.ds(first + j, count, stride=2 * detectors), :]
        imag_rows = spin_ref[0, pl.ds(first + j + detectors, count, stride=2 * detectors), :]
        rows = jnp.concatenate([real_rows, imag_rows], axis=0).astype(jnp.bfloat16)
        cycle = jnp.dot(rows, phase_ref[j], preferred_element_type=jnp.float32)
        total = jnp.zeros((ROWS, samples), jnp.float32)
        for g in range(blocks * groups):
            oc = outer_cos[g : g + 1]
            os = outer_sin[g : g + 1]
            real = cycle[g * ROWS : (g + 1) * ROWS]
            imag = cycle[count + g * ROWS : count + (g + 1) * ROWS]
            total += real * (oc * base_cos - os * base_sin)
            total -= imag * (os * base_cos + oc * base_sin)
        out_ref[pl.ds(j, 1), :] = before_ref[pl.ds(j, 1), :] + jnp.sum(total, axis=0, keepdims=True)


def body(wigner, sky_blocks, beam, block_order, pointing):
    device = lax.axis_index("sky")
    blocks, cycles, spins, block_size, degrees = wigner.shape
    degrees_here = beam.shape[0]
    lanes = beam.shape[1] // spins
    detectors = lanes // 2
    cycle_pixels = 2 * degrees
    orient_bins = 4 * spins
    pairs = cycles * detectors
    samples = pointing.shape[1]
    chunk = spins // CHUNKS
    params = pltpu.CompilerParams(vmem_limit_bytes=VMEM_LIMIT)

    degree = jnp.arange(degrees, dtype=jnp.int32)
    own_blocks = lax.dynamic_slice_in_dim(block_order, device * blocks, blocks)
    order = own_blocks[:, None] * block_size + jnp.arange(block_size, dtype=jnp.int32)
    sky = jnp.where(degree >= order[:, None, :, None], sky_blocks, jnp.bfloat16(0))

    points = lax.all_gather(pointing, "sky", axis=0, tiled=True)
    turned = jnp.transpose(beam.reshape(degrees_here, lanes, spins), (2, 0, 1))
    here = device * degrees_here + jnp.arange(degrees_here, dtype=jnp.int32)
    k_index = jnp.arange(spins, dtype=jnp.int32)
    turned = jnp.where(here[None, :, None] >= k_index[:, None, None], turned, jnp.bfloat16(0))

    gathered = [
        lax.all_gather(turned[c * chunk : (c + 1) * chunk], "sky", axis=0, tiled=False)
        for c in range(CHUNKS)
    ]

    phases, orients = pl.pallas_call(
        functools.partial(phase_kernel, cycle_pixels, orient_bins),
        grid=(pairs // ROWS,),
        in_specs=[pl.BlockSpec((ROWS, samples), lambda p: (p, 0))],
        out_specs=[
            pl.BlockSpec((ROWS, 2 * block_size, samples), lambda p: (p, 0, 0)),
            pl.BlockSpec((ROWS, 2 * ROWS, samples), lambda p: (p, 0, 0)),
        ],
        out_shape=[
            jax.ShapeDtypeStruct((pairs, 2 * block_size, samples), jnp.bfloat16),
            jax.ShapeDtypeStruct((pairs, 2 * ROWS, samples), jnp.float32),
        ],
        compiler_params=params,
        cost_estimate=pl.CostEstimate(flops=10**10, bytes_accessed=5 * 10**7, transcendentals=0),
        name="phases",
    )(points)

    count = blocks * chunk * lanes
    stream = jnp.zeros((pairs, samples), jnp.float32)
    for c in range(CHUNKS):
        first_k = c * chunk
        spin_sums = pl.pallas_call(
            functools.partial(spin_kernel, first_k),
            grid=(chunk,),
            in_specs=[
                pl.BlockSpec(memory_space=pltpu.SMEM),
                pl.BlockSpec(
                    (blocks, cycles, 1, block_size, degrees),
                    lambda k, first_k=first_k: (0, 0, first_k + k, 0, 0),
                ),
                pl.BlockSpec((blocks, 2, block_size, degrees), lambda k: (0, 0, 0, 0)),
                pl.BlockSpec(
                    (degrees // degrees_here, 1, degrees_here, lanes), lambda k: (0, k, 0, 0)
                ),
            ],
            out_specs=pl.BlockSpec(
                (cycles, blocks, 1, lanes, 2 * block_size), lambda k: (0, 0, k, 0, 0)
            ),
            out_shape=jax.ShapeDtypeStruct(
                (cycles, blocks, chunk, lanes, 2 * block_size), jnp.float32
            ),
            scratch_shapes=[
                pltpu.VMEM((2 * blocks * cycles * block_size, degrees), jnp.bfloat16)
            ],
            compiler_params=params,
            cost_estimate=pl.CostEstimate(
                flops=4 * 10**9, bytes_accessed=2 * 10**7, transcendentals=0
            ),
            name=f"spin_{c}",
        )(own_blocks, wigner, sky, gathered[c])
        spin_sums = spin_sums.reshape(cycles, count, 2 * block_size)
        row_of = lambda r, e: (r * (detectors // ROWS) + e, 0)
        pair_of = lambda r, e: (r * (detectors // ROWS) + e, 0, 0)
        stream = pl.pallas_call(
            functools.partial(
                stream_kernel, first_k, chunk, cycle_pixels, orient_bins, detectors, block_size
            ),
            grid=(cycles, detectors // ROWS),
            in_specs=[
                pl.BlockSpec(memory_space=pltpu.SMEM),
                pl.BlockSpec((1, count, 2 * block_size), lambda r, e: (r, 0, 0)),
                pl.BlockSpec((ROWS, 2 * block_size, samples), pair_of),
                pl.BlockSpec((ROWS, 2 * ROWS, samples), pair_of),
                pl.BlockSpec((ROWS, samples), row_of),
                pl.BlockSpec((ROWS, samples), row_of),
            ],
            out_specs=pl.BlockSpec((ROWS, samples), row_of),
            out_shape=jax.ShapeDtypeStruct((pairs, samples), jnp.float32),
            compiler_params=params,
            cost_estimate=pl.CostEstimate(
                flops=6 * 10**9, bytes_accessed=4 * 10**7, transcendentals=0
            ),
            name=f"stream_{c}",
        )(own_blocks, spin_sums, phases, orients, points, stream)

    return lax.psum_scatter(stream, "sky", scatter_dimension=0, tiled=True)


def solution(mesh):
    return jax.shard_map(
        body,
        mesh=mesh,
        in_specs=(
            P("sky", None, None, None, None),
            P("sky", None, None, None),
            P("sky", "groups"),
            P(),
            P(("groups", "sky"), None),
        ),
        out_specs=P(("groups", "sky"), None),
        check_vma=False,
    )
```

```python
import functools
import math

import jax
import jax.numpy as jnp
from jax import lax
from jax.experimental import pallas as pl
from jax.experimental.pallas import tpu as pltpu
from jax.sharding import PartitionSpec as P

ROWS = 8
VMEM_LIMIT = 48 * 1024 * 1024


def sincos(index, period):
    quarter = period // 4
    index = index & (period - 1)
    shifted = index + quarter // 2
    quadrant = (shifted >> (quarter.bit_length() - 1)) & 3
    rest = (shifted & (quarter - 1)) - quarter // 2
    x = rest.astype(jnp.float32) * (2.0 * math.pi / period)
    y = x * x
    s = x * (1.0 + y * (-1.0 / 6 + y * (1.0 / 120 + y * (-1.0 / 5040 + y * (1.0 / 362880)))))
    c = 1.0 + y * (-0.5 + y * (1.0 / 24 + y * (-1.0 / 720 + y * (1.0 / 40320))))
    odd = (quadrant & 1) == 1
    cos_size = jnp.where(odd, s, c)
    sin_size = jnp.where(odd, c, s)
    cos_value = jnp.where((quadrant == 1) | (quadrant == 2), -cos_size, cos_size)
    sin_value = jnp.where(quadrant >= 2, -sin_size, sin_size)
    return cos_value, sin_value


def phase_kernel(cycle_pixels, orient_bins, pointing_ref, phase_ref, orient_ref):
    samples = pointing_ref.shape[1]
    block_size = phase_ref.shape[1] // 2
    step = cycle_pixels // orient_bins
    low = lax.broadcasted_iota(jnp.int32, (ROWS, samples), 0)
    for j in range(pointing_ref.shape[0]):
        point = pointing_ref[pl.ds(j, 1), :]
        pixel = jnp.broadcast_to(point // orient_bins, (ROWS, samples))
        orient = jnp.broadcast_to(point & (orient_bins - 1), (ROWS, samples))
        base_cos, base_sin = sincos(low * pixel, cycle_pixels)
        if block_size == ROWS:
            cos_rows = [base_cos]
            sin_rows = [base_sin]
        else:
            cos_rows = []
            sin_rows = []
            outer_cos, outer_sin = sincos(low * ROWS * pixel, cycle_pixels)
            for a in range(block_size // ROWS):
                oc = outer_cos[a : a + 1]
                os = outer_sin[a : a + 1]
                cos_rows.append(oc * base_cos - os * base_sin)
                sin_rows.append(os * base_cos + oc * base_sin)
        phase_ref[j] = jnp.concatenate(cos_rows + sin_rows, axis=0).astype(jnp.bfloat16)
        orient_cos, orient_sin = sincos(low * orient * step, cycle_pixels)
        orient_ref[j] = jnp.concatenate([orient_cos, orient_sin], axis=0)


def spin_kernel(first_k, order_ref, wigner_ref, sky_ref, beam_ref, out_ref, coeff):
    blocks, cycles, _, block_size, degrees = wigner_ref.shape
    lanes = beam_ref.shape[-1]
    half = blocks * cycles * block_size
    for b in range(blocks):
        for r in range(cycles):
            table = wigner_ref[b, r, 0]
            row = (b * cycles + r) * block_size
            for c in range(2):
                coeff[c * half + row : c * half + row + block_size, :] = table * sky_ref[b, c]
    beam = beam_ref[...].reshape(degrees, lanes)
    sums = jnp.dot(coeff[...], beam, preferred_element_type=jnp.float32)
    sign = jnp.where(
        lax.broadcasted_iota(jnp.int32, (half, lanes), 1) < lanes // 2, -1.0, 1.0
    ).astype(jnp.float32)
    spin = sums[:half] + sign * pltpu.roll(sums[half:], lanes // 2, 1)
    spin = spin.astype(jnp.bfloat16).astype(jnp.float32)
    k_weight = jnp.where(first_k + pl.program_id(0) == 0, 1.0, 2.0).astype(jnp.float32)
    turned = sign * pltpu.roll(spin, lanes // 2, 1)
    slot = lax.broadcasted_iota(jnp.int32, (block_size, lanes), 0)
    for b in range(blocks):
        weight = jnp.where(order_ref[b] * block_size + slot == 0, 1.0, 2.0) * k_weight
        for r in range(cycles):
            row = (b * cycles + r) * block_size
            both = jnp.concatenate(
                [spin[row : row + block_size] * weight, turned[row : row + block_size] * weight],
                axis=0,
            )
            out_ref[r, b, 0] = both.T


def stream_kernel(chunks, cycle_pixels, orient_bins, detectors, block_size, order_ref, *refs):
    spin_refs = refs[: len(chunks)]
    phase_ref, orient_ref, pointing_ref, out_ref = refs[len(chunks) :]
    samples = pointing_ref.shape[1]
    blocks = order_ref.shape[0]
    step = cycle_pixels // orient_bins
    first = pl.program_id(1) * pointing_ref.shape[0]
    outer = [
        (b, first_k + a * ROWS)
        for first_k, size in chunks
        for b in range(blocks)
        for a in range(size // ROWS)
    ]
    row_id = lax.broadcasted_iota(jnp.int32, (max(ROWS, len(outer)), samples), 0)
    k_outer = jnp.zeros_like(row_id)
    m_outer = jnp.zeros_like(row_id)
    for g, (b, k) in enumerate(outer):
        k_outer = jnp.where(row_id == g, k * step, k_outer)
        m_outer = jnp.where(row_id == g, order_ref[b] * block_size, m_outer)
    for j in range(pointing_ref.shape[0]):
        point = pointing_ref[pl.ds(j, 1), :]
        pixel = point // orient_bins
        orient = point & (orient_bins - 1)
        outer_cos, outer_sin = sincos(k_outer * orient + m_outer * pixel, cycle_pixels)
        base_cos = orient_ref[j, :ROWS]
        base_sin = orient_ref[j, ROWS:]
        pieces = []
        for part in range(2):
            for (_, size), spin_ref in zip(chunks, spin_refs):
                start = first + j + part * detectors
                pieces.append(
                    spin_ref[0, pl.ds(start, blocks * size, stride=2 * detectors), :]
                )
        rows = jnp.concatenate(pieces, axis=0).astype(jnp.bfloat16)
        cycle = jnp.dot(rows, phase_ref[j], preferred_element_type=jnp.float32)
        imag_at = rows.shape[0] // 2
        total = jnp.zeros((ROWS, samples), jnp.float32)
        for g in range(len(outer)):
            oc = outer_cos[g : g + 1]
            os = outer_sin[g : g + 1]
            real = cycle[g * ROWS : (g + 1) * ROWS]
            imag = cycle[imag_at + g * ROWS : imag_at + (g + 1) * ROWS]
            total += oc * (real * base_cos - imag * base_sin)
            total -= os * (real * base_sin + imag * base_cos)
        out_ref[pl.ds(j, 1), :] = jnp.sum(total, axis=0, keepdims=True)


def body(wigner, sky_blocks, beam, block_order, pointing):
    device = lax.axis_index("sky")
    blocks, cycles, spins, block_size, degrees = wigner.shape
    degrees_here = beam.shape[0]
    lanes = beam.shape[1] // spins
    detectors = lanes // 2
    cycle_pixels = 2 * degrees
    orient_bins = 4 * spins
    pairs = cycles * detectors
    samples = pointing.shape[1]
    last = spins // 4
    chunks = [(0, spins - last), (spins - last, last)]
    params = pltpu.CompilerParams(vmem_limit_bytes=VMEM_LIMIT)

    degree = jnp.arange(degrees, dtype=jnp.int32)
    own_blocks = lax.dynamic_slice_in_dim(block_order, device * blocks, blocks)
    order = own_blocks[:, None] * block_size + jnp.arange(block_size, dtype=jnp.int32)
    sky = jnp.where(degree >= order[:, None, :, None], sky_blocks, jnp.bfloat16(0))

    points = lax.all_gather(pointing, "sky", axis=0, tiled=True)
    turned = jnp.transpose(beam.reshape(degrees_here, lanes, spins), (2, 0, 1))
    here = device * degrees_here + jnp.arange(degrees_here, dtype=jnp.int32)
    k_index = jnp.arange(spins, dtype=jnp.int32)
    turned = jnp.where(here[None, :, None] >= k_index[:, None, None], turned, jnp.bfloat16(0))

    gathered = []
    for first_k, size in chunks:
        piece = turned[first_k : first_k + size].reshape(size * degrees_here, lanes)
        if gathered:
            piece, gathered[-1] = lax.optimization_barrier((piece, gathered[-1]))
        whole = lax.all_gather(piece, "sky", axis=0, tiled=True)
        gathered.append(whole.reshape(degrees // degrees_here, size, degrees_here, lanes))

    phases, orients = pl.pallas_call(
        functools.partial(phase_kernel, cycle_pixels, orient_bins),
        grid=(pairs // ROWS,),
        in_specs=[pl.BlockSpec((ROWS, samples), lambda p: (p, 0))],
        out_specs=[
            pl.BlockSpec((ROWS, 2 * block_size, samples), lambda p: (p, 0, 0)),
            pl.BlockSpec((ROWS, 2 * ROWS, samples), lambda p: (p, 0, 0)),
        ],
        out_shape=[
            jax.ShapeDtypeStruct((pairs, 2 * block_size, samples), jnp.bfloat16),
            jax.ShapeDtypeStruct((pairs, 2 * ROWS, samples), jnp.float32),
        ],
        compiler_params=params,
        cost_estimate=pl.CostEstimate(flops=10**10, bytes_accessed=5 * 10**7, transcendentals=0),
        name="phases",
    )(points)

    spin_parts = []
    for c, (first_k, size) in enumerate(chunks):
        spin_parts.append(
            pl.pallas_call(
                functools.partial(spin_kernel, first_k),
                grid=(size,),
                in_specs=[
                    pl.BlockSpec(memory_space=pltpu.SMEM),
                    pl.BlockSpec(
                        (blocks, cycles, 1, block_size, degrees),
                        lambda k, first_k=first_k: (0, 0, first_k + k, 0, 0),
                    ),
                    pl.BlockSpec((blocks, 2, block_size, degrees), lambda k: (0, 0, 0, 0)),
                    pl.BlockSpec(
                        (degrees // degrees_here, 1, degrees_here, lanes),
                        lambda k: (0, k, 0, 0),
                    ),
                ],
                out_specs=pl.BlockSpec(
                    (cycles, blocks, 1, lanes, 2 * block_size), lambda k: (0, 0, k, 0, 0)
                ),
                out_shape=jax.ShapeDtypeStruct(
                    (cycles, blocks, size, lanes, 2 * block_size), jnp.float32
                ),
                scratch_shapes=[
                    pltpu.VMEM((2 * blocks * cycles * block_size, degrees), jnp.bfloat16)
                ],
                compiler_params=params,
                cost_estimate=pl.CostEstimate(
                    flops=10**9 * size, bytes_accessed=2 * 10**6 * size, transcendentals=0
                ),
                name=f"spin_{c}",
            )(own_blocks, wigner, sky, gathered[c]).reshape(
                cycles, blocks * size * lanes, 2 * block_size
            )
        )
    row_of = lambda r, e: (r * (detectors // ROWS) + e, 0)
    pair_of = lambda r, e: (r * (detectors // ROWS) + e, 0, 0)
    stream = pl.pallas_call(
        functools.partial(
            stream_kernel, chunks, cycle_pixels, orient_bins, detectors, block_size
        ),
        grid=(cycles, detectors // ROWS),
        in_specs=[pl.BlockSpec(memory_space=pltpu.SMEM)]
        + [
            pl.BlockSpec((1,) + part.shape[1:], lambda r, e: (r, 0, 0)) for part in spin_parts
        ]
        + [
            pl.BlockSpec((ROWS, 2 * block_size, samples), pair_of),
            pl.BlockSpec((ROWS, 2 * ROWS, samples), pair_of),
            pl.BlockSpec((ROWS, samples), row_of),
        ],
        out_specs=pl.BlockSpec((ROWS, samples), row_of),
        out_shape=jax.ShapeDtypeStruct((pairs, samples), jnp.float32),
        compiler_params=params,
        cost_estimate=pl.CostEstimate(flops=2 * 10**10, bytes_accessed=5 * 10**7, transcendentals=0),
        name="stream",
    )(own_blocks, *spin_parts, phases, orients, points)

    owners = pairs // pointing.shape[0]
    parts = lax.all_to_all(
        stream.reshape(owners, pointing.shape[0], samples), "sky", split_axis=0, concat_axis=0
    )
    return jnp.sum(parts, axis=0)


def solution(mesh):
    return jax.shard_map(
        body,
        mesh=mesh,
        in_specs=(
            P("sky", None, None, None, None),
            P("sky", None, None, None),
            P("sky", "groups"),
            P(),
            P(("groups", "sky"), None),
        ),
        out_specs=P(("groups", "sky"), None),
        check_vma=False,
    )
```

```python
import functools
import math

import jax
import jax.numpy as jnp
from jax import lax
from jax.experimental import pallas as pl
from jax.experimental.pallas import tpu as pltpu
from jax.sharding import PartitionSpec as P

ROWS = 8
VMEM_LIMIT = 48 * 1024 * 1024


def sincos(index, period):
    quarter = period // 4
    index = index & (period - 1)
    shifted = index + quarter // 2
    quadrant = (shifted >> (quarter.bit_length() - 1)) & 3
    rest = (shifted & (quarter - 1)) - quarter // 2
    x = rest.astype(jnp.float32) * (2.0 * math.pi / period)
    y = x * x
    s = x * (1.0 + y * (-1.0 / 6 + y * (1.0 / 120 + y * (-1.0 / 5040 + y * (1.0 / 362880)))))
    c = 1.0 + y * (-0.5 + y * (1.0 / 24 + y * (-1.0 / 720 + y * (1.0 / 40320))))
    odd = (quadrant & 1) == 1
    cos_size = jnp.where(odd, s, c)
    sin_size = jnp.where(odd, c, s)
    cos_value = jnp.where((quadrant == 1) | (quadrant == 2), -cos_size, cos_size)
    sin_value = jnp.where(quadrant >= 2, -sin_size, sin_size)
    return cos_value, sin_value


def phase_kernel(
    cycle_pixels, orient_bins, spins, order_ref, pointing_ref, phase_ref, orient_ref
):
    samples = pointing_ref.shape[1]
    block_size = phase_ref.shape[1] // 2
    step = cycle_pixels // orient_bins
    low = lax.broadcasted_iota(jnp.int32, (ROWS, samples), 0)
    blocks = order_ref.shape[0]
    groups = spins // ROWS
    row_id = lax.broadcasted_iota(jnp.int32, (blocks * groups, samples), 0)
    k_outer = (row_id & (groups - 1)) * ROWS * step
    m_outer = jnp.zeros_like(row_id)
    for b in range(blocks):
        inside = (row_id >= b * groups) & (row_id < (b + 1) * groups)
        m_outer = jnp.where(inside, order_ref[b] * block_size, m_outer)
    for j in range(pointing_ref.shape[0]):
        point = pointing_ref[pl.ds(j, 1), :]
        pixel = jnp.broadcast_to(point // orient_bins, (ROWS, samples))
        orient = jnp.broadcast_to(point & (orient_bins - 1), (ROWS, samples))
        base_cos, base_sin = sincos(low * pixel, cycle_pixels)
        if block_size == ROWS:
            cos_rows = [base_cos]
            sin_rows = [base_sin]
        else:
            cos_rows = []
            sin_rows = []
            outer_cos, outer_sin = sincos(low * ROWS * pixel, cycle_pixels)
            for a in range(block_size // ROWS):
                oc = outer_cos[a : a + 1]
                os = outer_sin[a : a + 1]
                cos_rows.append(oc * base_cos - os * base_sin)
                sin_rows.append(os * base_cos + oc * base_sin)
        phase_ref[j] = jnp.concatenate(cos_rows + sin_rows, axis=0).astype(jnp.bfloat16)
        orient_cos, orient_sin = sincos(low * orient * step, cycle_pixels)
        turns = k_outer * (point & (orient_bins - 1)) + m_outer * (point // orient_bins)
        outer_cos, outer_sin = sincos(turns, cycle_pixels)
        orient_ref[j] = jnp.concatenate([orient_cos, orient_sin, outer_cos, outer_sin], axis=0)


def spin_kernel(first_k, order_ref, wigner_ref, sky_ref, beam_ref, out_ref, coeff):
    blocks, cycles, _, block_size, degrees = wigner_ref.shape
    lanes = beam_ref.shape[-1]
    half = blocks * cycles * block_size
    for b in range(blocks):
        for r in range(cycles):
            table = wigner_ref[b, r, 0]
            row = (b * cycles + r) * block_size
            for c in range(2):
                coeff[c * half + row : c * half + row + block_size, :] = table * sky_ref[b, c]
    beam = beam_ref[...].reshape(degrees, lanes)
    sums = jnp.dot(coeff[...], beam, preferred_element_type=jnp.float32)
    sign = jnp.where(
        lax.broadcasted_iota(jnp.int32, (half, lanes), 1) < lanes // 2, -1.0, 1.0
    ).astype(jnp.float32)
    spin = sums[:half] + sign * pltpu.roll(sums[half:], lanes // 2, 1)
    spin = spin.astype(jnp.bfloat16).astype(jnp.float32)
    k_weight = jnp.where(first_k + pl.program_id(0) == 0, 1.0, 2.0).astype(jnp.float32)
    turned = sign * pltpu.roll(spin, lanes // 2, 1)
    slot = lax.broadcasted_iota(jnp.int32, (block_size, lanes), 0)
    for b in range(blocks):
        weight = jnp.where(order_ref[b] * block_size + slot == 0, 1.0, 2.0) * k_weight
        for r in range(cycles):
            row = (b * cycles + r) * block_size
            both = jnp.concatenate(
                [spin[row : row + block_size] * weight, turned[row : row + block_size] * weight],
                axis=0,
            )
            out_ref[r, b, 0] = both.T


def stream_kernel(chunks, detectors, blocks, *refs):
    spin_refs = refs[: len(chunks)]
    phase_ref, orient_ref, out_ref, rows = refs[len(chunks) :]
    samples = out_ref.shape[1]
    spins = sum(size for _, size in chunks)
    count = blocks * spins
    outer = count // ROWS
    first = pl.program_id(1) * ROWS
    for j in range(ROWS):
        for part in range(2):
            start = first + j + part * detectors
            for (first_k, size), spin_ref in zip(chunks, spin_refs):
                for b in range(blocks):
                    rows[j % 2, pl.ds(part * count + b * spins + first_k, size), :] = spin_ref[
                        0, pl.ds(b * size * 2 * detectors + start, size, stride=2 * detectors), :
                    ]
        cycle = jnp.dot(
            rows[j % 2].astype(jnp.bfloat16), phase_ref[j], preferred_element_type=jnp.float32
        )
        base_cos = orient_ref[j, :ROWS]
        base_sin = orient_ref[j, ROWS : 2 * ROWS]
        total = jnp.zeros((ROWS, samples), jnp.float32)
        for g in range(outer):
            oc = orient_ref[j, pl.ds(2 * ROWS + g, 1), :]
            os = orient_ref[j, pl.ds(2 * ROWS + outer + g, 1), :]
            real = cycle[g * ROWS : (g + 1) * ROWS]
            imag = cycle[count + g * ROWS : count + (g + 1) * ROWS]
            total += oc * (real * base_cos - imag * base_sin)
            total -= os * (real * base_sin + imag * base_cos)
        out_ref[pl.ds(j, 1), :] = jnp.sum(total, axis=0, keepdims=True)


def body(wigner, sky_blocks, beam, block_order, pointing):
    device = lax.axis_index("sky")
    blocks, cycles, spins, block_size, degrees = wigner.shape
    degrees_here = beam.shape[0]
    lanes = beam.shape[1] // spins
    detectors = lanes // 2
    cycle_pixels = 2 * degrees
    orient_bins = 4 * spins
    pairs = cycles * detectors
    samples = pointing.shape[1]
    last = spins // 8
    chunks = [(0, spins - last), (spins - last, last)]
    params = pltpu.CompilerParams(vmem_limit_bytes=VMEM_LIMIT)

    degree = jnp.arange(degrees, dtype=jnp.int32)
    own_blocks = lax.dynamic_slice_in_dim(block_order, device * blocks, blocks)
    order = own_blocks[:, None] * block_size + jnp.arange(block_size, dtype=jnp.int32)
    sky = jnp.where(degree >= order[:, None, :, None], sky_blocks, jnp.bfloat16(0))

    points = lax.all_gather(pointing, "sky", axis=0, tiled=True)
    turned = jnp.transpose(beam.reshape(degrees_here, lanes, spins), (2, 0, 1))
    here = device * degrees_here + jnp.arange(degrees_here, dtype=jnp.int32)
    k_index = jnp.arange(spins, dtype=jnp.int32)
    turned = jnp.where(here[None, :, None] >= k_index[:, None, None], turned, jnp.bfloat16(0))

    table_rows = 2 * ROWS + 2 * blocks * (spins // ROWS)
    phases, orients = pl.pallas_call(
        functools.partial(phase_kernel, cycle_pixels, orient_bins, spins),
        grid=(pairs // ROWS,),
        in_specs=[
            pl.BlockSpec(memory_space=pltpu.SMEM),
            pl.BlockSpec((ROWS, samples), lambda p: (p, 0)),
        ],
        out_specs=[
            pl.BlockSpec((ROWS, 2 * block_size, samples), lambda p: (p, 0, 0)),
            pl.BlockSpec((ROWS, table_rows, samples), lambda p: (p, 0, 0)),
        ],
        out_shape=[
            jax.ShapeDtypeStruct((pairs, 2 * block_size, samples), jnp.bfloat16),
            jax.ShapeDtypeStruct((pairs, table_rows, samples), jnp.float32),
        ],
        compiler_params=params,
        cost_estimate=pl.CostEstimate(flops=10**10, bytes_accessed=5 * 10**7, transcendentals=0),
        name="phases",
    )(own_blocks, points)

    gathered = []
    for first_k, size in chunks:
        piece = turned[first_k : first_k + size].reshape(size * degrees_here, lanes)
        if gathered:
            piece, phases, orients = lax.optimization_barrier((piece, phases, orients))
            piece, gathered[-1] = lax.optimization_barrier((piece, gathered[-1]))
        whole = lax.all_gather(piece, "sky", axis=0, tiled=True)
        gathered.append(whole.reshape(degrees // degrees_here, size, degrees_here, lanes))

    spin_parts = []
    for c, (first_k, size) in enumerate(chunks):
        spin_parts.append(
            pl.pallas_call(
                functools.partial(spin_kernel, first_k),
                grid=(size,),
                in_specs=[
                    pl.BlockSpec(memory_space=pltpu.SMEM),
                    pl.BlockSpec(
                        (blocks, cycles, 1, block_size, degrees),
                        lambda k, first_k=first_k: (0, 0, first_k + k, 0, 0),
                    ),
                    pl.BlockSpec((blocks, 2, block_size, degrees), lambda k: (0, 0, 0, 0)),
                    pl.BlockSpec(
                        (degrees // degrees_here, 1, degrees_here, lanes),
                        lambda k: (0, k, 0, 0),
                    ),
                ],
                out_specs=pl.BlockSpec(
                    (cycles, blocks, 1, lanes, 2 * block_size), lambda k: (0, 0, k, 0, 0)
                ),
                out_shape=jax.ShapeDtypeStruct(
                    (cycles, blocks, size, lanes, 2 * block_size), jnp.float32
                ),
                scratch_shapes=[
                    pltpu.VMEM((2 * blocks * cycles * block_size, degrees), jnp.bfloat16)
                ],
                compiler_params=params,
                cost_estimate=pl.CostEstimate(
                    flops=10**9 * size, bytes_accessed=2 * 10**6 * size, transcendentals=0
                ),
                name=f"spin_{c}",
            )(own_blocks, wigner, sky, gathered[c]).reshape(
                cycles, blocks * size * lanes, 2 * block_size
            )
        )
    row_of = lambda r, e: (r * (detectors // ROWS) + e, 0)
    pair_of = lambda r, e: (r * (detectors // ROWS) + e, 0, 0)
    stream = pl.pallas_call(
        functools.partial(stream_kernel, chunks, detectors, blocks),
        grid=(cycles, detectors // ROWS),
        in_specs=[
            pl.BlockSpec((1,) + part.shape[1:], lambda r, e: (r, 0, 0)) for part in spin_parts
        ]
        + [
            pl.BlockSpec((ROWS, 2 * block_size, samples), pair_of),
            pl.BlockSpec((ROWS, table_rows, samples), pair_of),
        ],
        out_specs=pl.BlockSpec((ROWS, samples), row_of),
        out_shape=jax.ShapeDtypeStruct((pairs, samples), jnp.float32),
        scratch_shapes=[pltpu.VMEM((2, 2 * blocks * spins, 2 * block_size), jnp.float32)],
        compiler_params=params,
        cost_estimate=pl.CostEstimate(flops=2 * 10**10, bytes_accessed=5 * 10**7, transcendentals=0),
        name="stream",
    )(*spin_parts, phases, orients)

    owners = pairs // pointing.shape[0]
    parts = lax.all_to_all(
        stream.reshape(owners, pointing.shape[0], samples), "sky", split_axis=0, concat_axis=0
    )
    return jnp.sum(parts, axis=0)


def solution(mesh):
    return jax.shard_map(
        body,
        mesh=mesh,
        in_specs=(
            P("sky", None, None, None, None),
            P("sky", None, None, None),
            P("sky", "groups"),
            P(),
            P(("groups", "sky"), None),
        ),
        out_specs=P(("groups", "sky"), None),
        check_vma=False,
    )
```

```python
import functools
import math

import jax
import jax.numpy as jnp
from jax import lax
from jax.experimental import pallas as pl
from jax.experimental.pallas import tpu as pltpu
from jax.sharding import PartitionSpec as P

ROWS = 8
VMEM_LIMIT = 48 * 1024 * 1024


def sincos(index, period):
    quarter = period // 4
    index = index & (period - 1)
    shifted = index + quarter // 2
    quadrant = (shifted >> (quarter.bit_length() - 1)) & 3
    rest = (shifted & (quarter - 1)) - quarter // 2
    x = rest.astype(jnp.float32) * (2.0 * math.pi / period)
    y = x * x
    s = x * (1.0 + y * (-1.0 / 6 + y * (1.0 / 120 + y * (-1.0 / 5040 + y * (1.0 / 362880)))))
    c = 1.0 + y * (-0.5 + y * (1.0 / 24 + y * (-1.0 / 720 + y * (1.0 / 40320))))
    odd = (quadrant & 1) == 1
    cos_size = jnp.where(odd, s, c)
    sin_size = jnp.where(odd, c, s)
    cos_value = jnp.where((quadrant == 1) | (quadrant == 2), -cos_size, cos_size)
    sin_value = jnp.where(quadrant >= 2, -sin_size, sin_size)
    return cos_value, sin_value


def phase_kernel(
    cycle_pixels, orient_bins, spins, order_ref, pointing_ref, phase_ref, orient_ref
):
    samples = pointing_ref.shape[1]
    block_size = phase_ref.shape[1] // 2
    step = cycle_pixels // orient_bins
    low = lax.broadcasted_iota(jnp.int32, (ROWS, samples), 0)
    blocks = order_ref.shape[0]
    groups = spins // ROWS
    row_id = lax.broadcasted_iota(jnp.int32, (blocks * groups, samples), 0)
    k_outer = (row_id & (groups - 1)) * ROWS * step
    m_outer = jnp.zeros_like(row_id)
    for b in range(blocks):
        inside = (row_id >= b * groups) & (row_id < (b + 1) * groups)
        m_outer = jnp.where(inside, order_ref[b] * block_size, m_outer)
    for j in range(pointing_ref.shape[0]):
        point = pointing_ref[pl.ds(j, 1), :]
        pixel = jnp.broadcast_to(point // orient_bins, (ROWS, samples))
        orient = jnp.broadcast_to(point & (orient_bins - 1), (ROWS, samples))
        base_cos, base_sin = sincos(low * pixel, cycle_pixels)
        if block_size == ROWS:
            cos_rows = [base_cos]
            sin_rows = [base_sin]
        else:
            cos_rows = []
            sin_rows = []
            outer_cos, outer_sin = sincos(low * ROWS * pixel, cycle_pixels)
            for a in range(block_size // ROWS):
                oc = outer_cos[a : a + 1]
                os = outer_sin[a : a + 1]
                cos_rows.append(oc * base_cos - os * base_sin)
                sin_rows.append(os * base_cos + oc * base_sin)
        phase_ref[j] = jnp.concatenate(cos_rows + sin_rows, axis=0).astype(jnp.bfloat16)
        orient_cos, orient_sin = sincos(low * orient * step, cycle_pixels)
        turns = k_outer * (point & (orient_bins - 1)) + m_outer * (point // orient_bins)
        outer_cos, outer_sin = sincos(turns, cycle_pixels)
        orient_ref[j] = jnp.concatenate([orient_cos, orient_sin, outer_cos, outer_sin], axis=0)


def spin_kernel(first_k, order_ref, wigner_ref, sky_ref, beam_ref, out_ref, coeff):
    blocks, cycles, _, block_size, degrees = wigner_ref.shape
    lanes = beam_ref.shape[-1]
    half = blocks * cycles * block_size
    for b in range(blocks):
        for r in range(cycles):
            table = wigner_ref[b, r, 0]
            row = (b * cycles + r) * block_size
            for c in range(2):
                coeff[c * half + row : c * half + row + block_size, :] = table * sky_ref[b, c]
    beam = beam_ref[...].reshape(degrees, lanes)
    sums = jnp.dot(coeff[...], beam, preferred_element_type=jnp.float32)
    sign = jnp.where(
        lax.broadcasted_iota(jnp.int32, (half, lanes), 1) < lanes // 2, -1.0, 1.0
    ).astype(jnp.float32)
    spin = sums[:half] + sign * pltpu.roll(sums[half:], lanes // 2, 1)
    spin = spin.astype(jnp.bfloat16).astype(jnp.float32)
    k_weight = jnp.where(first_k + pl.program_id(0) == 0, 1.0, 2.0).astype(jnp.float32)
    turned = sign * pltpu.roll(spin, lanes // 2, 1)
    slot = lax.broadcasted_iota(jnp.int32, (block_size, lanes), 0)
    for b in range(blocks):
        weight = jnp.where(order_ref[b] * block_size + slot == 0, 1.0, 2.0) * k_weight
        for r in range(cycles):
            row = (b * cycles + r) * block_size
            both = jnp.concatenate(
                [spin[row : row + block_size] * weight, turned[row : row + block_size] * weight],
                axis=0,
            )
            out_ref[r, b, 0] = both.T


def stream_kernel(chunks, detectors, blocks, *refs):
    spin_refs = refs[: len(chunks)]
    phase_ref, orient_ref, out_ref, rows = refs[len(chunks) :]
    samples = out_ref.shape[1]
    spins = sum(size for _, size in chunks)
    count = blocks * spins
    outer = count // ROWS
    first = pl.program_id(1) * ROWS
    def add_pair(cycle, j):
        base_cos = orient_ref[j, :ROWS]
        base_sin = orient_ref[j, ROWS : 2 * ROWS]
        total = jnp.zeros((ROWS, samples), jnp.float32)
        for g in range(outer):
            oc = orient_ref[j, pl.ds(2 * ROWS + g, 1), :]
            os = orient_ref[j, pl.ds(2 * ROWS + outer + g, 1), :]
            real = cycle[g * ROWS : (g + 1) * ROWS]
            imag = cycle[count + g * ROWS : count + (g + 1) * ROWS]
            total += oc * (real * base_cos - imag * base_sin)
            total -= os * (real * base_sin + imag * base_cos)
        out_ref[pl.ds(j, 1), :] = jnp.sum(total, axis=0, keepdims=True)

    width = phase_ref.shape[1]
    pairs_each = 2
    for half in range(pairs_each):
        other = (1 - half) * width
        rows[:, pl.ds(half * 2 * count, 2 * count), pl.ds(other, width)] = jnp.zeros(
            (2, 2 * count, width), jnp.float32
        )
    for j in range(ROWS):
        half = j % pairs_each
        slot = (j // pairs_each) % 2
        base = half * 2 * count
        for part in range(2):
            start = first + j + part * detectors
            for (first_k, size), spin_ref in zip(chunks, spin_refs):
                for b in range(blocks):
                    rows[
                        slot,
                        pl.ds(base + part * count + b * spins + first_k, size),
                        pl.ds(half * width, width),
                    ] = spin_ref[
                        0, pl.ds(b * size * 2 * detectors + start, size, stride=2 * detectors), :
                    ]
        if half != pairs_each - 1:
            continue
        phases = phase_ref[j - 1 : j + 1].reshape(pairs_each * width, samples)
        both = jnp.dot(
            rows[slot].astype(jnp.bfloat16), phases, preferred_element_type=jnp.float32
        )
        for pair in range(pairs_each):
            at = j - 1 + pair
            add_pair(both[pair * 2 * count : (pair + 1) * 2 * count], at)


def body(wigner, sky_blocks, beam, block_order, pointing):
    device = lax.axis_index("sky")
    blocks, cycles, spins, block_size, degrees = wigner.shape
    degrees_here = beam.shape[0]
    lanes = beam.shape[1] // spins
    detectors = lanes // 2
    cycle_pixels = 2 * degrees
    orient_bins = 4 * spins
    pairs = cycles * detectors
    samples = pointing.shape[1]
    last = spins // 8
    chunks = [(0, spins - last), (spins - last, last)]
    params = pltpu.CompilerParams(vmem_limit_bytes=VMEM_LIMIT)

    degree = jnp.arange(degrees, dtype=jnp.int32)
    own_blocks = lax.dynamic_slice_in_dim(block_order, device * blocks, blocks)
    order = own_blocks[:, None] * block_size + jnp.arange(block_size, dtype=jnp.int32)
    sky = jnp.where(degree >= order[:, None, :, None], sky_blocks, jnp.bfloat16(0))

    points = lax.all_gather(pointing, "sky", axis=0, tiled=True)
    turned = jnp.transpose(beam.reshape(degrees_here, lanes, spins), (2, 0, 1))
    here = device * degrees_here + jnp.arange(degrees_here, dtype=jnp.int32)
    k_index = jnp.arange(spins, dtype=jnp.int32)
    turned = jnp.where(here[None, :, None] >= k_index[:, None, None], turned, jnp.bfloat16(0))

    table_rows = 2 * ROWS + 2 * blocks * (spins // ROWS)
    phases, orients = pl.pallas_call(
        functools.partial(phase_kernel, cycle_pixels, orient_bins, spins),
        grid=(pairs // ROWS,),
        in_specs=[
            pl.BlockSpec(memory_space=pltpu.SMEM),
            pl.BlockSpec((ROWS, samples), lambda p: (p, 0)),
        ],
        out_specs=[
            pl.BlockSpec((ROWS, 2 * block_size, samples), lambda p: (p, 0, 0)),
            pl.BlockSpec((ROWS, table_rows, samples), lambda p: (p, 0, 0)),
        ],
        out_shape=[
            jax.ShapeDtypeStruct((pairs, 2 * block_size, samples), jnp.bfloat16),
            jax.ShapeDtypeStruct((pairs, table_rows, samples), jnp.float32),
        ],
        compiler_params=params,
        cost_estimate=pl.CostEstimate(flops=10**10, bytes_accessed=5 * 10**7, transcendentals=0),
        name="phases",
    )(own_blocks, points)

    gathered = []
    for first_k, size in chunks:
        piece = turned[first_k : first_k + size].reshape(size * degrees_here, lanes)
        if gathered:
            piece, phases, orients = lax.optimization_barrier((piece, phases, orients))
            piece, gathered[-1] = lax.optimization_barrier((piece, gathered[-1]))
        whole = lax.all_gather(piece, "sky", axis=0, tiled=True)
        gathered.append(whole.reshape(degrees // degrees_here, size, degrees_here, lanes))

    spin_parts = []
    for c, (first_k, size) in enumerate(chunks):
        spin_parts.append(
            pl.pallas_call(
                functools.partial(spin_kernel, first_k),
                grid=(size,),
                in_specs=[
                    pl.BlockSpec(memory_space=pltpu.SMEM),
                    pl.BlockSpec(
                        (blocks, cycles, 1, block_size, degrees),
                        lambda k, first_k=first_k: (0, 0, first_k + k, 0, 0),
                    ),
                    pl.BlockSpec((blocks, 2, block_size, degrees), lambda k: (0, 0, 0, 0)),
                    pl.BlockSpec(
                        (degrees // degrees_here, 1, degrees_here, lanes),
                        lambda k: (0, k, 0, 0),
                    ),
                ],
                out_specs=pl.BlockSpec(
                    (cycles, blocks, 1, lanes, 2 * block_size), lambda k: (0, 0, k, 0, 0)
                ),
                out_shape=jax.ShapeDtypeStruct(
                    (cycles, blocks, size, lanes, 2 * block_size), jnp.float32
                ),
                scratch_shapes=[
                    pltpu.VMEM((2 * blocks * cycles * block_size, degrees), jnp.bfloat16)
                ],
                compiler_params=params,
                cost_estimate=pl.CostEstimate(
                    flops=10**9 * size, bytes_accessed=2 * 10**6 * size, transcendentals=0
                ),
                name=f"spin_{c}",
            )(own_blocks, wigner, sky, gathered[c]).reshape(
                cycles, blocks * size * lanes, 2 * block_size
            )
        )
    row_of = lambda r, e: (r * (detectors // ROWS) + e, 0)
    pair_of = lambda r, e: (r * (detectors // ROWS) + e, 0, 0)
    stream = pl.pallas_call(
        functools.partial(stream_kernel, chunks, detectors, blocks),
        grid=(cycles, detectors // ROWS),
        in_specs=[
            pl.BlockSpec((1,) + part.shape[1:], lambda r, e: (r, 0, 0)) for part in spin_parts
        ]
        + [
            pl.BlockSpec((ROWS, 2 * block_size, samples), pair_of),
            pl.BlockSpec((ROWS, table_rows, samples), pair_of),
        ],
        out_specs=pl.BlockSpec((ROWS, samples), row_of),
        out_shape=jax.ShapeDtypeStruct((pairs, samples), jnp.float32),
        scratch_shapes=[pltpu.VMEM((2, 4 * blocks * spins, 4 * block_size), jnp.float32)],
        compiler_params=params,
        cost_estimate=pl.CostEstimate(flops=2 * 10**10, bytes_accessed=5 * 10**7, transcendentals=0),
        name="stream",
    )(*spin_parts, phases, orients)

    owners = pairs // pointing.shape[0]
    parts = lax.all_to_all(
        stream.reshape(owners, pointing.shape[0], samples), "sky", split_axis=0, concat_axis=0
    )
    return jnp.sum(parts, axis=0)


def solution(mesh):
    return jax.shard_map(
        body,
        mesh=mesh,
        in_specs=(
            P("sky", None, None, None, None),
            P("sky", None, None, None),
            P("sky", "groups"),
            P(),
            P(("groups", "sky"), None),
        ),
        out_specs=P(("groups", "sky"), None),
        check_vma=False,
    )
```
